256 devices in a mesh: wide: 32 (over x, y, core), narrow: 8 (over z).
Axes of the slice: x: 4, y: 4, z: 8, core: 2. Of those that a mesh axis runs over, the one named last changes fastest.
Arguments:
- design: float32 [262144, 256], P(('wide', 'narrow')), as said below
- sign_flips: int32 [262144], P(('wide', 'narrow')), may hold values from -1 to 1, as said below
- sample_ids: int32 [1024], replicated, may hold values from 0 to 262143
Outputs:
- sketch: float32 [1024, 256], P(('wide', 'narrow'))
- gram_matrix: float32 [256, 256], replicated
The draws below stay inside these ranges and needn't reach their ends.
Inputs may be any that keep to these rules, and one draw needn't show every extreme that they name: `sign_flips`: each entry is +1 or -1. `design`: real-valued entries of varying row and column scales.
All inputs are finite; a program needn't handle non-finite values.
Results may differ from the reference program's by a relative error of at most 0.00012.
Values sent between devices are 32-bit elements; how exact they have to be, the bound alone decides.
A program may use at most 64 MiB of HBM per device.

```python
import math
import jax
import jax.numpy as jnp
from jax import lax

D = 256
ROWS = 262144
SAMPLES = 1024


def draw_design(key, part):
    key = jax.random.fold_in(key, 11)
    first, second, third = jax.random.split(key, 3)
    values = jax.random.normal(first, (ROWS, D), jnp.float32)
    row_scale = jnp.exp(jax.random.uniform(second, (ROWS, 1), jnp.float32) * math.log(10.0))
    col_scale = jnp.exp(jax.random.uniform(third, (1, D), jnp.float32) * math.log(10.0))
    return 0.1 * values * row_scale * col_scale


def draw_sign_flips(key, part):
    key = jax.random.fold_in(key, 23)
    return jax.random.randint(key, (ROWS,), 0, 2, jnp.int32) * 2 - 1


def set_ends(entries, rng, low, high):
    spot = [jax.random.randint(jax.random.fold_in(rng, axis), (), 0, length) for axis, length in enumerate(entries.shape)]
    longest = entries.shape.index(max(entries.shape))
    neighbour = spot[:longest] + [(spot[longest] + 1) % entries.shape[longest]] + spot[longest + 1:]
    return entries.at[tuple(spot)].set(low).at[tuple(neighbour)].set(high)


def setup_inputs(seed: int = 0) -> dict:
    streams_of = jax.random.split(jax.random.key(seed), 4)
    return {
        "design": draw_design(jax.random.fold_in(streams_of[3], 71), 0),
        "sign_flips": draw_sign_flips(jax.random.fold_in(streams_of[3], 71), 0),
        "sample_ids": set_ends(jax.random.randint(streams_of[2], (SAMPLES,), 0, ROWS), jax.random.fold_in(streams_of[2], 1), 0, ROWS - 1).astype(jnp.int32),
    }


def hadamard(values):
    length, features = values.shape
    half = 1
    while half < length:
        blocks = values.reshape(-1, 2, half, features)
        values = jnp.stack((blocks[:, 0] + blocks[:, 1], blocks[:, 0] - blocks[:, 1]), axis=1).reshape(length, features)
        half = half * 2
    return values

def reference(design, sign_flips, sample_ids):
    flipped = design * sign_flips.astype(jnp.float32)[:, None]
    mixed = hadamard(flipped) / math.sqrt(ROWS)
    sketch = jnp.take(mixed, sample_ids, axis=0)
    gram_matrix = jnp.dot(sketch.T, sketch, precision=lax.Precision.HIGHEST) / SAMPLES
    return (sketch, gram_matrix)
```

```python
import functools

import jax
import jax.numpy as jnp
from jax import lax
from jax.experimental import pallas as pl
from jax.experimental.pallas import tpu as pltpu
from jax.sharding import PartitionSpec as P

MESH = pl.DeviceIdType.MESH
FAR_FIRST = (2, 1, 3, 0)
Z_ORDER = (4, 3, 5, 2, 6, 1, 7)
BF16, F32, I32 = jnp.bfloat16, jnp.float32, jnp.int32


def contract_rows(a, b):
    return lax.dot_general(a, b, (((0,), (0,)), ((), ())), preferred_element_type=F32)


def kernel(
    design, flips, ids, sketch_out, gram_out,
    rows_in, rows_hi, rows_lo, bits, masks, part, from_sib, chip_sum,
    plane_in, plane_sum, line_in, gathered, gram_own, gram_sib,
    load_sem, sib_send, sib_recv, plane_send, plane_recv, line_send, line_recv,
    gather_send, gather_recv, gram_send, gram_recv,
):
    wide, z = lax.axis_index("wide"), lax.axis_index("narrow")
    core = lax.rem(wide, 2)
    square = lax.div(wide, 2)
    x, y = lax.div(square, 4), lax.rem(square, 4)
    device = wide * 8 + z

    load = pltpu.make_async_copy(design, rows_in, load_sem)
    load.start()

    def wrap(v, n):
        return lax.rem(v, n)

    plane = [(dx, dy) for dx in FAR_FIRST for dy in FAR_FIRST if dx or dy]

    def plane_square(dx, dy):
        return wrap(x + dx, 4) * 4 + wrap(y + dy, 4)

    sibling = (wide + 1 - 2 * core, z)
    line = [(dz, dc) for dz in Z_ORDER for dc in (0, 1)]

    barrier = pltpu.get_barrier_semaphore()
    for dz, dc in line:
        target = (square * 2 + wrap(core + dc, 2), wrap(z + dz, 8))
        pl.semaphore_signal(barrier, inc=1, device_id=target, device_id_type=MESH)
    for dx, dy in plane:
        target = (plane_square(dx, dy) * 2 + core, z)
        pl.semaphore_signal(barrier, inc=1, device_id=target, device_id_type=MESH)
    pl.semaphore_signal(barrier, inc=1, device_id=sibling, device_id_type=MESH)

    bit = lax.broadcasted_iota(I32, (32, 1024), 0)
    bits[...] = (lax.shift_right_logical(jnp.broadcast_to(ids[...], (32, 1024)), bit) & 1).astype(F32).astype(BF16)
    bit = lax.broadcasted_iota(I32, (32, 512), 0)
    lane = lax.broadcasted_iota(I32, (32, 512), 1)
    block, low = lax.shift_right_logical(lane, 7), lane & 127
    of_low = lax.shift_right_logical(low, jnp.minimum(bit, 7)) & 1
    of_device = lax.shift_right_logical(jnp.full((32, 512), device, I32), jnp.maximum(bit - 10, 0)) & 1
    of_device = jnp.where(bit >= 10, of_device, 0)
    first = jnp.where(bit < 7, of_low, of_device)
    masks[...] = jnp.where(block == 0, first, jnp.where(bit == 6 + block, 1, 0)).astype(F32).astype(BF16)

    load.wait()
    scaled = rows_in[...] * (1.0 / 512.0)
    hi = scaled.astype(BF16)
    rows_hi[...] = hi
    rows_lo[...] = (scaled - hi.astype(F32)).astype(BF16)
    flip = flips[...].astype(F32).astype(BF16)

    def local(m, _):
        span = pl.ds(pl.multiple_of(m * 256, 256), 256)
        counts = contract_rows(bits[:, span], masks[...])
        base = (1 - 2 * (counts[:, :128].astype(I32) & 1)).astype(F32).astype(BF16)
        by_bit = [(1.0 - 2.0 * counts[:, 128 * j : 128 * j + 128]).astype(BF16) for j in (1, 2, 3)]
        signs = [base]
        for j in range(3):
            signs = signs + [s * by_bit[j] for s in signs]
        signs = [s * jnp.broadcast_to(flip[:, 128 * k : 128 * k + 128], (256, 128)) for k, s in enumerate(signs)]
        table = jnp.concatenate(signs, axis=1)
        got = jnp.dot(table, rows_hi[...], preferred_element_type=F32)
        got = got + jnp.dot(table, rows_lo[...], preferred_element_type=F32)
        part[0, m] = got[:, :128]
        part[1, m] = got[:, 128:]
        return 0

    lax.fori_loop(0, 4, local, 0)
    pl.semaphore_wait(barrier, len(line) + len(plane) + 1)

    halves = []
    for k, dx in enumerate(FAR_FIRST):
        m = wrap(x + dx, 4)
        copy = pltpu.make_async_remote_copy(
            part.at[1 - core, m], from_sib.at[m], sib_send.at[k], sib_recv.at[k], device_id=sibling, device_id_type=MESH
        )
        copy.start()
        halves.append(copy)
    sent = []
    for k, dx in enumerate(FAR_FIRST):
        m = wrap(x + dx, 4)
        halves[k].wait_recv()
        chip_sum[pl.ds(m * 4, 4)] = (part[core, m] + from_sib[m]).reshape(4, 64, 128)
        for dy in FAR_FIRST:
            if dx or dy:
                there = plane_square(dx, dy)
                n = len(sent)
                copy = pltpu.make_async_remote_copy(
                    chip_sum.at[there], plane_in.at[n], plane_send.at[n], plane_recv.at[n],
                    device_id=(there * 2 + core, z), device_id_type=MESH,
                )
                copy.start()
                sent.append(copy)
    total = chip_sum[square]
    for n in reversed(range(15)):
        sent[n].wait_recv()
        total = total + plane_in[n]
    plane_sum[...] = total.reshape(2, 32, 128)

    along = []
    for n, (dz, dc) in enumerate(line + [(0, 1)]):
        to_core = wrap(core + dc, 2)
        copy = pltpu.make_async_remote_copy(
            plane_sum.at[to_core], line_in.at[z, core], line_send.at[n], line_recv.at[n],
            device_id=(square * 2 + to_core, wrap(z + dz, 8)), device_id_type=MESH,
        )
        copy.start()
        along.append(copy)
    line_in[z, core] = plane_sum[core]
    for copy in reversed(along):
        copy.wait_recv()
    for h in range(2):
        total = line_in[0, h]
        for k in range(1, 8):
            total = total + line_in[k, h]
        gathered[square, :, 128 * h : 128 * h + 128] = total

    round_sent = []
    for n, (dx, dy) in enumerate(plane):
        copy = pltpu.make_async_remote_copy(
            gathered.at[square], gathered.at[square], gather_send.at[n], gather_recv.at[n],
            device_id=(plane_square(dx, dy) * 2 + core, z), device_id_type=MESH,
        )
        copy.start()
        round_sent.append(copy)
    pair = gathered[square, pl.ds(pl.multiple_of(lax.div(z, 2) * 8, 8), 8)]
    sketch_out[...] = jnp.where(lax.rem(z, 2) == 0, pair[:4], pair[4:])
    for copy in halves + sent + along:
        copy.wait_send()
    for copy in reversed(round_sent):
        copy.wait_recv()

    rows = gathered[...].reshape(512, 256)
    hi = rows.astype(BF16)
    lo = (rows - hi.astype(F32)).astype(BF16)
    cross = contract_rows(hi, lo)
    gram = contract_rows(hi, hi) + (cross + cross.T)
    gram_own[...] = gram * (1.0 / 1024.0)
    copy = pltpu.make_async_remote_copy(
        gram_own, gram_sib, gram_send, gram_recv, device_id=sibling, device_id_type=MESH
    )
    copy.start()
    copy.wait()
    gram_out[...] = gram_own[...] + gram_sib[...]
    for copy in round_sent:
        copy.wait_send()


def on_device(design, sign_flips, sample_ids):
    dma = pltpu.SemaphoreType.DMA
    vmem = pl.BlockSpec(memory_space=pltpu.VMEM)
    return pl.pallas_call(
        kernel,
        out_shape=(jax.ShapeDtypeStruct((4, 256), F32), jax.ShapeDtypeStruct((256, 256), F32)),
        in_specs=[pl.BlockSpec(memory_space=pl.ANY), vmem, vmem],
        out_specs=(vmem, vmem),
        scratch_shapes=[
            pltpu.VMEM((1024, 256), F32),
            pltpu.VMEM((1024, 256), BF16),
            pltpu.VMEM((1024, 256), BF16),
            pltpu.VMEM((32, 1024), BF16),
            pltpu.VMEM((32, 512), BF16),
            pltpu.VMEM((2, 4, 256, 128), F32),
            pltpu.VMEM((4, 256, 128), F32),
            pltpu.VMEM((16, 64, 128), F32),
            pltpu.VMEM((15, 64, 128), F32),
            pltpu.VMEM((2, 32, 128), F32),
            pltpu.VMEM((8, 2, 32, 128), F32),
            pltpu.VMEM((16, 32, 256), F32),
            pltpu.VMEM((256, 256), F32),
            pltpu.VMEM((256, 256), F32),
            dma, dma((4,)), dma((4,)), dma((15,)), dma((15,)), dma((15,)), dma((15,)),
            dma((15,)), dma((15,)), dma, dma,
        ],
        compiler_params=pltpu.CompilerParams(collective_id=0, has_side_effects=True, vmem_limit_bytes=48 << 20),
    )(design, sign_flips.reshape(1, 1024), sample_ids.reshape(1, 1024))


def solution(mesh):
    placed = (P(("wide", "narrow"), None), P(("wide", "narrow")), P())
    return jax.shard_map(
        on_device,
        mesh=mesh,
        in_specs=placed,
        out_specs=(P(("wide", "narrow"), None), P()),
        check_vma=False,
    )
```

```python
import functools

import jax
import jax.numpy as jnp
from jax import lax
from jax.experimental import pallas as pl
from jax.experimental.pallas import tpu as pltpu
from jax.sharding import PartitionSpec as P

MESH = pl.DeviceIdType.MESH
PARTS = 4
PART_ROWS = 64 // PARTS
PAIR, PLANE_SUM, LINE_SUM, ROUND, HALF = range(5)
PLANE = (
    (2, 2), (1, 2), (2, 1), (3, 2), (2, 3), (1, 1), (3, 3), (1, 3), (3, 1), (0, 2), (2, 0), (0, 1), (1, 0), (0, 3), (3, 0),
)
LINE = (4, 3, 5, 2, 6, 1, 7)
BF16, F32, I32 = jnp.bfloat16, jnp.float32, jnp.int32


def contract_rows(a, b):
    return lax.dot_general(a, b, (((0,), (0,)), ((), ())), preferred_element_type=F32)


def split(values):
    hi = values.astype(BF16)
    return hi, (values - hi.astype(F32)).astype(BF16)


def kernel(
    design, flips, ids, sketch_out, gram_out,
    rows_in, flips_in, ids_in, rows_hi, rows_lo, signs, mine, partner, from_partner, chip_sum, plane_in, line_in, gathered,
    load_sem, send_sem, recv_sem,
):
    wide, z = lax.axis_index("wide"), lax.axis_index("narrow")
    core, square = lax.rem(wide, 2), lax.div(wide, 2)
    x, y = lax.div(square, 4), lax.rem(square, 4)
    device = wide * 8 + z
    load_ids = pltpu.make_async_copy(ids, ids_in, load_sem.at[0])
    load_ids.start()
    load = pltpu.make_async_copy(design, rows_in, load_sem.at[1])
    load.start()
    load_flips = pltpu.make_async_copy(flips, flips_in, load_sem.at[2])
    load_flips.start()

    squares = [lax.rem(x + dx, 4) * 4 + lax.rem(y + dy, 4) for dx, dy in PLANE]
    plane = [(there * 2 + core, z) for there in squares]
    line = [(wide, lax.rem(z + dz, 8)) for dz in LINE]
    sibling = (wide + 1 - 2 * core, z)
    barrier = pltpu.get_barrier_semaphore()
    peers = plane + line + [sibling]
    for peer in peers:
        pl.semaphore_signal(barrier, inc=1, device_id=peer, device_id_type=MESH)

    def copy_of(step, a, source, target, peer):
        return pltpu.make_async_remote_copy(
            source, target, send_sem.at[step, a], recv_sem.at[step, a], device_id=peer, device_id_type=MESH
        )

    bit = lax.broadcasted_iota(I32, (32, 512), 0)
    lane = lax.broadcasted_iota(I32, (32, 512), 1)
    block, low = lax.shift_right_logical(lane, 7), lane & 127
    of_low = lax.shift_right_logical(low, jnp.minimum(bit, 7)) & 1
    of_device = lax.shift_right_logical(jnp.full((32, 512), device, I32), jnp.maximum(bit - 10, 0)) & 1
    of_device = jnp.where(bit >= 10, of_device, 0)
    first = jnp.where(bit < 7, of_low, of_device)
    masks = jnp.where(block == 0, first, jnp.where(bit == 6 + block, 1, 0)).astype(F32).astype(BF16)
    load_ids.wait()
    bit = lax.broadcasted_iota(I32, (32, 1024), 0)
    bits = (lax.shift_right_logical(jnp.broadcast_to(ids_in[...], (32, 1024)), bit) & 1).astype(F32).astype(BF16)
    counts = contract_rows(bits, masks)
    base = (1 - 2 * (counts[:, :128].astype(I32) & 1)).astype(F32)
    signs[0] = base.astype(BF16).reshape(16, PARTS, PART_ROWS, 128)
    for j in (1, 2, 3):
        signs[j] = (1.0 - 2.0 * counts[:, 128 * j : 128 * j + 128]).astype(BF16).reshape(16, PARTS, PART_ROWS, 128)

    load_flips.wait()
    flip = flips_in[...].astype(F32).astype(BF16)
    load.wait()
    hi, lo = split(rows_in[...] * (1.0 / 512.0))
    rows_hi[...] = hi
    rows_lo[...] = lo

    for a in range(PARTS):
        table = [signs[0, :, a].reshape(16 * PART_ROWS, 128)]
        for j in (1, 2, 3):
            other = signs[j, :, a].reshape(16 * PART_ROWS, 128)
            table = table + [s * other for s in table]
        table = [s * jnp.broadcast_to(flip[:, 128 * k : 128 * k + 128], (16 * PART_ROWS, 128)) for k, s in enumerate(table)]
        table = jnp.concatenate(table, axis=1)
        got = jnp.dot(table, rows_hi[...], preferred_element_type=F32)
        got = got + jnp.dot(table, rows_lo[...], preferred_element_type=F32)
        left, right = got[:, :128].reshape(16, PART_ROWS, 128), got[:, 128:].reshape(16, PART_ROWS, 128)
        mine[a] = jnp.where(core == 0, left, right)
        partner[a] = jnp.where(core == 0, right, left)
        if a == 0:
            pl.semaphore_wait(barrier, len(peers))
        copy_of(PAIR, a, partner.at[a], from_partner.at[a], sibling).start()

    def all_of(step, a):
        whole = (
            from_partner.at[a], plane_in.at[a], line_in.at[a, pl.ds(0, 7)],
            gathered.at[0, a, pl.ds(0, 15)], gathered.at[0, a],
        )[step]
        return copy_of(step, a, whole, whole, sibling)

    for a in range(PARTS):
        all_of(PAIR, a).wait_recv()
        chip_sum[a] = mine[a] + from_partner[a]
        for n in range(15):
            copy_of(PLANE_SUM, a, chip_sum.at[a, squares[n]], plane_in.at[a, n], plane[n]).start()
    for a in range(PARTS):
        all_of(PLANE_SUM, a).wait_recv()
        total = chip_sum[a, square]
        for n in range(15):
            total = total + plane_in[a, n]
        line_in[a, z] = total
        here = line_in.at[a, z]
        for n in range(7):
            copy_of(LINE_SUM, a, here, here, line[n]).start()
    for a in range(PARTS):
        all_of(LINE_SUM, a).wait_recv()
        total = line_in[a, 0]
        for k in range(1, 8):
            total = total + line_in[a, k]
        gathered[core, a, square] = total
        here = gathered.at[core, a, square]
        for n in range(15):
            copy_of(ROUND, a, here, here, plane[n]).start()
    for a in range(PARTS):
        all_of(ROUND, a).wait_recv()
        here = gathered.at[core, a]
        copy_of(HALF, a, here, here, sibling).start()
    gram = None
    for a in range(PARTS):
        all_of(HALF, a).wait_recv()
        left, right = gathered[0, a].reshape(16 * PART_ROWS, 128), gathered[1, a].reshape(16 * PART_ROWS, 128)
        hi, lo = split(jnp.concatenate([left, right], axis=1))
        cross = contract_rows(hi, lo)
        term = contract_rows(hi, hi) + (cross + cross.T)
        gram = term if gram is None else gram + term
    gram_out[...] = gram * (1.0 / 1024.0)
    row = core * 32 + z * 4
    part, row = lax.div(row, PART_ROWS), lax.rem(row, PART_ROWS)
    tile = pl.ds(pl.multiple_of(lax.div(row, 8) * 8, 8), 8)
    for h in range(2):
        eight = gathered[h, part, square, tile]
        sketch_out[:, 128 * h : 128 * h + 128] = jnp.where(lax.rem(z, 2) == 0, eight[:4], eight[4:])
    for step in range(5):
        for a in range(PARTS):
            all_of(step, a).wait_send()


def on_device(design, sign_flips, sample_ids):
    dma = pltpu.SemaphoreType.DMA
    vmem, hbm = pl.BlockSpec(memory_space=pltpu.VMEM), pl.BlockSpec(memory_space=pltpu.HBM)
    return pl.pallas_call(
        kernel,
        out_shape=(jax.ShapeDtypeStruct((4, 256), F32), jax.ShapeDtypeStruct((256, 256), F32)),
        in_specs=[hbm, hbm, hbm],
        out_specs=(vmem, vmem),
        scratch_shapes=[
            pltpu.VMEM((1024, 256), F32),
            pltpu.VMEM((1, 1024), I32),
            pltpu.VMEM((1, 1024), I32),
            pltpu.VMEM((1024, 256), BF16),
            pltpu.VMEM((1024, 256), BF16),
            pltpu.VMEM((4, 16, PARTS, PART_ROWS, 128), BF16),
            pltpu.VMEM((PARTS, 16, PART_ROWS, 128), F32),
            pltpu.VMEM((PARTS, 16, PART_ROWS, 128), F32),
            pltpu.VMEM((PARTS, 16, PART_ROWS, 128), F32),
            pltpu.VMEM((PARTS, 16, PART_ROWS, 128), F32),
            pltpu.VMEM((PARTS, 15, PART_ROWS, 128), F32),
            pltpu.VMEM((PARTS, 8, PART_ROWS, 128), F32),
            pltpu.VMEM((2, PARTS, 16, PART_ROWS, 128), F32),
            dma((3,)), dma((5, PARTS)), dma((5, PARTS)),
        ],
        compiler_params=pltpu.CompilerParams(collective_id=0, has_side_effects=True, vmem_limit_bytes=40 << 20),
    )(*[pltpu.with_memory_space_constraint(v, pltpu.HBM) for v in (design, sign_flips.reshape(1, 1024), sample_ids.reshape(1, 1024))])


def solution(mesh):
    placed = (P(("wide", "narrow"), None), P(("wide", "narrow")), P())
    return jax.shard_map(
        on_device,
        mesh=mesh,
        in_specs=placed,
        out_specs=(P(("wide", "narrow"), None), P()),
        check_vma=False,
    )
```

```python
import functools

import jax
import jax.numpy as jnp
from jax import lax
from jax.experimental import pallas as pl
from jax.experimental.pallas import tpu as pltpu
from jax.sharding import PartitionSpec as P

MESH = pl.DeviceIdType.MESH
PARTS, LEVEL_PART = 4, 1
SQUARE_ROWS, LEVEL_ROWS = 16, 32
SQUARE_PARTS = [a for a in range(PARTS) if a != LEVEL_PART]
PAIR, SUM, ACROSS, ROUND, HALF = range(5)
PLANE = (
    (2, 2), (1, 2), (2, 1), (3, 2), (2, 3), (1, 1), (3, 3), (1, 3), (3, 1), (0, 2), (2, 0), (0, 1), (1, 0), (0, 3), (3, 0),
)
LINE = (4, 3, 5, 2, 6, 1, 7)
BF16, F32, I32 = jnp.bfloat16, jnp.float32, jnp.int32


def contract_rows(a, b):
    return lax.dot_general(a, b, (((0,), (0,)), ((), ())), preferred_element_type=F32)


def split(values):
    hi = values.astype(BF16)
    return hi, (values - hi.astype(F32)).astype(BF16)


def kernel(
    design, flips, ids, sketch_out, gram_out,
    rows_in, flips_in, ids_in, rows_hi, rows_lo, square_signs, level_signs, mine, partner, from_partner, chip_sum,
    plane_in, line_across, line_in, plane_across, gathered,
    load_sem, send_sem, recv_sem,
):
    wide, z = lax.axis_index("wide"), lax.axis_index("narrow")
    core, square = lax.rem(wide, 2), lax.div(wide, 2)
    x, y = lax.div(square, 4), lax.rem(square, 4)
    device = wide * 8 + z
    load_ids = pltpu.make_async_copy(ids, ids_in, load_sem.at[0])
    load_ids.start()
    load = pltpu.make_async_copy(design, rows_in, load_sem.at[1])
    load.start()
    load_flips = pltpu.make_async_copy(flips, flips_in, load_sem.at[2])
    load_flips.start()

    squares = [lax.rem(x + dx, 4) * 4 + lax.rem(y + dy, 4) for dx, dy in PLANE]
    plane = [(there * 2 + core, z) for there in squares]
    levels = [lax.rem(z + dz, 8) for dz in LINE]
    line = [(wide, there) for there in levels]
    sibling = (wide + 1 - 2 * core, z)
    barrier = pltpu.get_barrier_semaphore()
    peers = plane + line + [sibling]
    for peer in peers:
        pl.semaphore_signal(barrier, inc=1, device_id=peer, device_id_type=MESH)

    def copy_of(step, a, source, target, peer):
        return pltpu.make_async_remote_copy(
            source, target, send_sem.at[step, a], recv_sem.at[step, a], device_id=peer, device_id_type=MESH
        )

    bit = lax.broadcasted_iota(I32, (32, 512), 0)
    lane = lax.broadcasted_iota(I32, (32, 512), 1)
    block, low = lax.shift_right_logical(lane, 7), lane & 127
    of_low = lax.shift_right_logical(low, jnp.minimum(bit, 7)) & 1
    of_device = lax.shift_right_logical(jnp.full((32, 512), device, I32), jnp.maximum(bit - 10, 0)) & 1
    of_device = jnp.where(bit >= 10, of_device, 0)
    first = jnp.where(bit < 7, of_low, of_device)
    masks = jnp.where(block == 0, first, jnp.where(bit == 6 + block, 1, 0)).astype(F32).astype(BF16)
    load_ids.wait()
    bit = lax.broadcasted_iota(I32, (32, 1024), 0)
    bits = (lax.shift_right_logical(jnp.broadcast_to(ids_in[...], (32, 1024)), bit) & 1).astype(F32).astype(BF16)
    counts = contract_rows(bits, masks)
    base = (1 - 2 * (counts[:, :128].astype(I32) & 1)).astype(F32)
    for j in range(4):
        sign = (base if j == 0 else 1.0 - 2.0 * counts[:, 128 * j : 128 * j + 128]).astype(BF16)
        square_signs[j] = sign[:768].reshape(16, 3, SQUARE_ROWS, 128)
        level_signs[j] = sign[768:]

    load_flips.wait()
    flip = flips_in[...].astype(F32).astype(BF16)
    load.wait()
    hi, lo = split(rows_in[...] * (1.0 / 512.0))
    rows_hi[...] = hi
    rows_lo[...] = lo

    def signs_of(a, j):
        if a == LEVEL_PART:
            return level_signs[j]
        return square_signs[j, :, SQUARE_PARTS.index(a)].reshape(256, 128)

    for a in range(PARTS):
        table = [signs_of(a, 0)]
        for j in (1, 2, 3):
            other = signs_of(a, j)
            table = table + [s * other for s in table]
        table = [s * jnp.broadcast_to(flip[:, 128 * k : 128 * k + 128], (256, 128)) for k, s in enumerate(table)]
        table = jnp.concatenate(table, axis=1)
        got = jnp.dot(table, rows_hi[...], preferred_element_type=F32)
        got = got + jnp.dot(table, rows_lo[...], preferred_element_type=F32)
        left, right = got[:, :128], got[:, 128:]
        mine[a] = jnp.where(core == 0, left, right)
        partner[a] = jnp.where(core == 0, right, left)
    pl.semaphore_wait(barrier, len(peers))
    for a in range(PARTS):
        copy_of(PAIR, a, partner.at[a], from_partner.at[a], sibling).start()

    def of_square(there):
        return pl.ds(pl.multiple_of(there * SQUARE_ROWS, 8), SQUARE_ROWS)

    def of_level(there):
        return pl.ds(pl.multiple_of(there * LEVEL_ROWS, 8), LEVEL_ROWS)

    def all_of(step, a):
        if step == PAIR:
            whole = from_partner.at[a]
        elif step == HALF:
            whole = gathered.at[0, a]
        elif a == LEVEL_PART:
            whole = (line_in, plane_across.at[pl.ds(0, 15)], gathered.at[0, a, pl.ds(0, 7 * LEVEL_ROWS)])[step - SUM]
        else:
            b = SQUARE_PARTS.index(a)
            whole = (
                plane_in.at[b], line_across.at[b, pl.ds(0, 7)], gathered.at[0, a, pl.ds(0, 15 * SQUARE_ROWS)]
            )[step - SUM]
        return copy_of(step, a, whole, whole, sibling)

    for a in range(PARTS):
        all_of(PAIR, a).wait_recv()
        chip_sum[a] = mine[a] + from_partner[a]
        if a == LEVEL_PART:
            for n in range(7):
                copy_of(SUM, a, chip_sum.at[a, of_level(levels[n])], line_in.at[n], line[n]).start()
        else:
            b = SQUARE_PARTS.index(a)
            for n in range(15):
                copy_of(SUM, a, chip_sum.at[a, of_square(squares[n])], plane_in.at[b, n], plane[n]).start()
    for a in range(PARTS):
        all_of(SUM, a).wait_recv()
        if a == LEVEL_PART:
            total = chip_sum[a, of_level(z)]
            for n in range(7):
                total = total + line_in[n]
            plane_across[square] = total
            here = plane_across.at[square]
            for n in range(15):
                copy_of(ACROSS, a, here, here, plane[n]).start()
        else:
            b = SQUARE_PARTS.index(a)
            total = chip_sum[a, of_square(square)]
            for n in range(15):
                total = total + plane_in[b, n]
            line_across[b, z] = total
            here = line_across.at[b, z]
            for n in range(7):
                copy_of(ACROSS, a, here, here, line[n]).start()
    for a in range(PARTS):
        all_of(ACROSS, a).wait_recv()
        if a == LEVEL_PART:
            terms, own, others = [plane_across[k] for k in range(16)], of_level(z), line
        else:
            b = SQUARE_PARTS.index(a)
            terms, own, others = [line_across[b, k] for k in range(8)], of_square(square), plane
        total = terms[0]
        for term in terms[1:]:
            total = total + term
        gathered[core, a, own] = total
        here = gathered.at[core, a, own]
        for peer in others:
            copy_of(ROUND, a, here, here, peer).start()
    for a in range(PARTS):
        all_of(ROUND, a).wait_recv()
        here = gathered.at[core, a]
        copy_of(HALF, a, here, here, sibling).start()
    gram = None
    for a in range(PARTS):
        all_of(HALF, a).wait_recv()
        left, right = gathered[0, a], gathered[1, a]
        hi, lo = split(jnp.concatenate([left, right], axis=1))
        cross = contract_rows(hi, lo)
        term = contract_rows(hi, hi) + (cross + cross.T)
        gram = term if gram is None else gram + term
    gram_out[...] = gram * (1.0 / 1024.0)
    row = device * 4
    b = lax.div(lax.rem(row, 48), 16)
    in_square = lax.div(row, 48) * SQUARE_ROWS + lax.rem(row, 16)
    part = jnp.where(row < 768, jnp.where(b >= LEVEL_PART, b + 1, b), LEVEL_PART)
    tile = pl.ds(pl.multiple_of(lax.div(jnp.where(row < 768, in_square, row - 768), 8) * 8, 8), 8)
    for h in range(2):
        eight = gathered[h, part, tile]
        sketch_out[:, 128 * h : 128 * h + 128] = jnp.where(lax.rem(z, 2) == 0, eight[:4], eight[4:])
    for step in range(5):
        for a in range(PARTS):
            all_of(step, a).wait_send()


def on_device(design, sign_flips, sample_ids):
    dma = pltpu.SemaphoreType.DMA
    vmem, hbm = pl.BlockSpec(memory_space=pltpu.VMEM), pl.BlockSpec(memory_space=pltpu.HBM)
    sketch, gram = pl.pallas_call(
        kernel,
        out_shape=(pltpu.VMEM((4, 256), F32), pltpu.VMEM((256, 256), F32)),
        in_specs=[hbm, hbm, hbm],
        out_specs=(vmem, vmem),
        scratch_shapes=[
            pltpu.VMEM((1024, 256), F32),
            pltpu.VMEM((1, 1024), I32),
            pltpu.VMEM((1, 1024), I32),
            pltpu.VMEM((1024, 256), BF16),
            pltpu.VMEM((1024, 256), BF16),
            pltpu.VMEM((4, 16, 3, SQUARE_ROWS, 128), BF16),
            pltpu.VMEM((4, 256, 128), BF16),
            pltpu.VMEM((PARTS, 256, 128), F32),
            pltpu.VMEM((PARTS, 256, 128), F32),
            pltpu.VMEM((PARTS, 256, 128), F32),
            pltpu.VMEM((PARTS, 256, 128), F32),
            pltpu.VMEM((3, 15, SQUARE_ROWS, 128), F32),
            pltpu.VMEM((3, 8, SQUARE_ROWS, 128), F32),
            pltpu.VMEM((7, LEVEL_ROWS, 128), F32),
            pltpu.VMEM((16, LEVEL_ROWS, 128), F32),
            pltpu.VMEM((2, PARTS, 256, 128), F32),
            dma((3,)), dma((5, PARTS)), dma((5, PARTS)),
        ],
        compiler_params=pltpu.CompilerParams(collective_id=0, has_side_effects=True, vmem_limit_bytes=40 << 20),
    )(*[pltpu.with_memory_space_constraint(v, pltpu.HBM) for v in (design, sign_flips.reshape(1, 1024), sample_ids.reshape(1, 1024))])
    return pl.pallas_call(
        hand_out,
        out_shape=(jax.ShapeDtypeStruct((4, 256), F32), jax.ShapeDtypeStruct((256, 256), F32)),
        in_specs=[vmem, vmem],
        out_specs=(hbm, hbm),
        scratch_shapes=[dma((2,))],
    )(pltpu.with_memory_space_constraint(sketch, pltpu.VMEM), pltpu.with_memory_space_constraint(gram, pltpu.VMEM))


def hand_out(sketch, gram, sketch_out, gram_out, sem):
    first = pltpu.make_async_copy(gram, gram_out, sem.at[0])
    second = pltpu.make_async_copy(sketch, sketch_out, sem.at[1])
    first.start()
    second.start()
    first.wait()
    second.wait()


def solution(mesh):
    placed = (P(("wide", "narrow"), None), P(("wide", "narrow")), P())
    return jax.shard_map(
        on_device,
        mesh=mesh,
        in_specs=placed,
        out_specs=(P(("wide", "narrow"), None), P()),
        check_vma=False,
    )
```

```python
import functools

import jax
import jax.numpy as jnp
from jax import lax
from jax.experimental import pallas as pl
from jax.experimental.pallas import tpu as pltpu
from jax.sharding import PartitionSpec as P

MESH = pl.DeviceIdType.MESH
PARTS, LEVEL_PART = 4, 1
SQUARE_ROWS, LEVEL_ROWS = 16, 32
SQUARE_PARTS = [a for a in range(PARTS) if a != LEVEL_PART]
ORDER = tuple((stage, a) for stage in range(3) for a in range(PARTS))
PAIR, SUM, ACROSS, ROUND, HALF = range(5)
PLANE = (
    (2, 2), (1, 2), (2, 1), (3, 2), (2, 3), (1, 1), (3, 3), (1, 3), (3, 1), (0, 2), (2, 0), (0, 1), (1, 0), (0, 3), (3, 0),
)
BY_START = tuple(sorted(range(16), key=lambda q: (min(q // 4, 4 - q // 4) + min(q % 4, 4 - q % 4), q)))
LINE = (4, 3, 5, 2, 6, 1, 7)
BF16, F32, I32 = jnp.bfloat16, jnp.float32, jnp.int32


def contract_rows(a, b):
    return lax.dot_general(a, b, (((0,), (0,)), ((), ())), preferred_element_type=F32)


def split(values):
    hi = values.astype(BF16)
    return hi, (values - hi.astype(F32)).astype(BF16)


def kernel(
    design, flips, ids, sketch_out, gram_out,
    rows_in, flips_in, ids_in, rows_hi, rows_lo, square_signs, level_signs, mine, partner, from_partner, all_sums,
    plane_in, line_across, line_in, plane_across, gathered,
    load_sem, send_sem, recv_sem,
):
    wide, z = lax.axis_index("wide"), lax.axis_index("narrow")
    core, square = lax.rem(wide, 2), lax.div(wide, 2)
    x, y = lax.div(square, 4), lax.rem(square, 4)
    device = wide * 8 + z
    load_ids = pltpu.make_async_copy(ids, ids_in, load_sem.at[0])
    load_ids.start()
    load = pltpu.make_async_copy(design, rows_in, load_sem.at[1])
    load.start()
    load_flips = pltpu.make_async_copy(flips, flips_in, load_sem.at[2])
    load_flips.start()

    squares = [lax.rem(x + dx, 4) * 4 + lax.rem(y + dy, 4) for dx, dy in PLANE]
    plane = [(there * 2 + core, z) for there in squares]
    levels = [lax.rem(z + dz, 8) for dz in LINE]
    line = [(wide, there) for there in levels]
    sibling = (wide + 1 - 2 * core, z)
    rank = sum(jnp.where(square == there, p, 0) for p, there in enumerate(BY_START))
    early_squares = [jnp.where(k < rank, BY_START[k], BY_START[k + 1]) for k in range(15)]
    early_plane = [(there * 2 + core, z) for there in early_squares]
    early_line = [(wide, jnp.where(k < z, k, k + 1)) for k in range(7)]
    barrier = pltpu.get_barrier_semaphore()
    peers = plane + line + [sibling]
    for peer in peers:
        pl.semaphore_signal(barrier, inc=1, device_id=peer, device_id_type=MESH)

    def copy_of(step, a, source, target, peer):
        return pltpu.make_async_remote_copy(
            source, target, send_sem.at[step], recv_sem.at[step, a], device_id=peer, device_id_type=MESH
        )

    bit = lax.broadcasted_iota(I32, (32, 512), 0)
    lane = lax.broadcasted_iota(I32, (32, 512), 1)
    block, low = lax.shift_right_logical(lane, 7), lane & 127
    of_low = lax.shift_right_logical(low, jnp.minimum(bit, 7)) & 1
    of_device = lax.shift_right_logical(jnp.full((32, 512), device, I32), jnp.maximum(bit - 10, 0)) & 1
    of_device = jnp.where(bit >= 10, of_device, 0)
    first = jnp.where(bit < 7, of_low, of_device)
    masks = jnp.where(block == 0, first, jnp.where(bit == 6 + block, 1, 0)).astype(F32).astype(BF16)
    load_ids.wait()
    bit = lax.broadcasted_iota(I32, (32, 1024), 0)
    bits = (lax.shift_right_logical(jnp.broadcast_to(ids_in[...], (32, 1024)), bit) & 1).astype(F32).astype(BF16)
    counts = contract_rows(bits, masks)
    base = (1 - 2 * (counts[:, :128].astype(I32) & 1)).astype(F32)
    for j in range(4):
        sign = (base if j == 0 else 1.0 - 2.0 * counts[:, 128 * j : 128 * j + 128]).astype(BF16)
        square_signs[j] = sign[:768].reshape(16, 3, SQUARE_ROWS, 128)
        level_signs[j] = sign[768:]

    load_flips.wait()
    flip = flips_in[...].astype(F32).astype(BF16)
    load.wait()
    hi, lo = split(rows_in[...] * (1.0 / 512.0))
    rows_hi[...] = hi
    rows_lo[...] = lo

    def signs_of(a, j):
        if a == LEVEL_PART:
            return level_signs[j]
        return square_signs[j, :, SQUARE_PARTS.index(a)].reshape(256, 128)

    for a in range(PARTS):
        table = [signs_of(a, 0)]
        for j in (1, 2, 3):
            other = signs_of(a, j)
            table = table + [s * other for s in table]
        table = [s * jnp.broadcast_to(flip[:, 128 * k : 128 * k + 128], (256, 128)) for k, s in enumerate(table)]
        table = jnp.concatenate(table, axis=1)
        got = jnp.dot(table, rows_hi[...], preferred_element_type=F32)
        got = got + jnp.dot(table, rows_lo[...], preferred_element_type=F32)
        left, right = got[:, :128], got[:, 128:]
        mine[a] = jnp.where(core == 0, left, right)
        partner[a] = jnp.where(core == 0, right, left)
    pl.semaphore_wait(barrier, len(peers))
    for a in range(PARTS):
        copy_of(PAIR, a, partner.at[a], from_partner.at[a], sibling).start()

    def of_square(there, first=0):
        return pl.ds(pl.multiple_of(first + there * SQUARE_ROWS, 8), SQUARE_ROWS)

    def of_level(there, first=0):
        return pl.ds(pl.multiple_of(first + there * LEVEL_ROWS, 8), LEVEL_ROWS)

    def all_of(step, a):
        if step == PAIR:
            whole = from_partner.at[a]
        elif step == HALF:
            whole = gathered.at[0, a]
        elif a == LEVEL_PART:
            whole = (line_in, plane_across.at[pl.ds(0, 15)], gathered.at[0, a, pl.ds(0, 7 * LEVEL_ROWS)])[step - SUM]
        else:
            b = SQUARE_PARTS.index(a)
            whole = (
                plane_in.at[b], line_across.at[b, pl.ds(0, 7)], gathered.at[0, a, pl.ds(0, 15 * SQUARE_ROWS)]
            )[step - SUM]
        return copy_of(step, a, whole, whole, sibling)

    for a in range(PARTS):
        all_of(PAIR, a).wait_recv()
        all_sums[pl.ds(256 * a, 256)] = mine[a] + from_partner[a]
        if a == LEVEL_PART:
            for n in range(7):
                copy_of(SUM, a, all_sums.at[of_level(levels[n], 256 * a)], line_in.at[n], line[n]).start()
        else:
            b = SQUARE_PARTS.index(a)
            for n in range(15):
                copy_of(SUM, a, all_sums.at[of_square(squares[n], 256 * a)], plane_in.at[b, n], plane[n]).start()
    def add_up(a):
        all_of(SUM, a).wait_recv()
        if a == LEVEL_PART:
            total = all_sums[of_level(z, 256 * a)]
            for n in range(7):
                total = total + line_in[n]
            plane_across[square] = total
            here = plane_across.at[square]
            for n in range(15):
                copy_of(ACROSS, a, here, here, plane[n]).start()
        else:
            b = SQUARE_PARTS.index(a)
            total = all_sums[of_square(square, 256 * a)]
            for n in range(15):
                total = total + plane_in[b, n]
            line_across[b, z] = total
            here = line_across.at[b, z]
            for n in range(7):
                copy_of(ACROSS, a, here, here, early_line[n]).start()

    def add_across(a):
        all_of(ACROSS, a).wait_recv()
        if a == LEVEL_PART:
            terms, own, others = [plane_across[k] for k in range(16)], of_level(z), early_line
        else:
            b = SQUARE_PARTS.index(a)
            terms, own, others = [line_across[b, k] for k in range(8)], of_square(square), early_plane
        total = terms[0]
        for term in terms[1:]:
            total = total + term
        gathered[core, a, own] = total
        here = gathered.at[core, a, own]
        for peer in others:
            copy_of(ROUND, a, here, here, peer).start()

    def pass_on(a):
        all_of(ROUND, a).wait_recv()
        here = gathered.at[core, a]
        copy_of(HALF, a, here, here, sibling).start()

    for stage, a in ORDER:
        (add_up, add_across, pass_on)[stage](a)
    gram = None
    for a in range(PARTS):
        all_of(HALF, a).wait_recv()
        left, right = gathered[0, a], gathered[1, a]
        hi, lo = split(jnp.concatenate([left, right], axis=1))
        cross = contract_rows(hi, lo)
        term = contract_rows(hi, hi) + (cross + cross.T)
        gram = term if gram is None else gram + term
    gram_out[...] = gram * (1.0 / 1024.0)
    row = device * 4
    b = lax.div(lax.rem(row, 48), 16)
    in_square = lax.div(row, 48) * SQUARE_ROWS + lax.rem(row, 16)
    part = jnp.where(row < 768, jnp.where(b >= LEVEL_PART, b + 1, b), LEVEL_PART)
    tile = pl.ds(pl.multiple_of(lax.div(jnp.where(row < 768, in_square, row - 768), 8) * 8, 8), 8)
    for h in range(2):
        eight = gathered[h, part, tile]
        sketch_out[:, 128 * h : 128 * h + 128] = jnp.where(lax.rem(z, 2) == 0, eight[:4], eight[4:])
    for step, rows in enumerate((1024, 944, 816, 944, 1024)):
        whole = all_sums.at[pl.ds(0, rows)]
        copy_of(step, 0, whole, whole, sibling).wait_send()


def on_device(design, sign_flips, sample_ids):
    dma = pltpu.SemaphoreType.DMA
    vmem, hbm = pl.BlockSpec(memory_space=pltpu.VMEM), pl.BlockSpec(memory_space=pltpu.HBM)
    sketch, gram = pl.pallas_call(
        kernel,
        out_shape=(pltpu.VMEM((4, 256), F32), pltpu.VMEM((256, 256), F32)),
        in_specs=[hbm, hbm, hbm],
        out_specs=(vmem, vmem),
        scratch_shapes=[
            pltpu.VMEM((1024, 256), F32),
            pltpu.VMEM((1, 1024), I32),
            pltpu.VMEM((1, 1024), I32),
            pltpu.VMEM((1024, 256), BF16),
            pltpu.VMEM((1024, 256), BF16),
            pltpu.VMEM((4, 16, 3, SQUARE_ROWS, 128), BF16),
            pltpu.VMEM((4, 256, 128), BF16),
            pltpu.VMEM((PARTS, 256, 128), F32),
            pltpu.VMEM((PARTS, 256, 128), F32),
            pltpu.VMEM((PARTS, 256, 128), F32),
            pltpu.VMEM((1024, 128), F32),
            pltpu.VMEM((3, 15, SQUARE_ROWS, 128), F32),
            pltpu.VMEM((3, 8, SQUARE_ROWS, 128), F32),
            pltpu.VMEM((7, LEVEL_ROWS, 128), F32),
            pltpu.VMEM((16, LEVEL_ROWS, 128), F32),
            pltpu.VMEM((2, PARTS, 256, 128), F32),
            dma((3,)), dma((5,)), dma((5, PARTS)),
        ],
        compiler_params=pltpu.CompilerParams(collective_id=0, has_side_effects=True, vmem_limit_bytes=40 << 20),
    )(*[pltpu.with_memory_space_constraint(v, pltpu.HBM) for v in (design, sign_flips.reshape(1, 1024), sample_ids.reshape(1, 1024))])
    return pl.pallas_call(
        hand_out,
        out_shape=(jax.ShapeDtypeStruct((4, 256), F32), jax.ShapeDtypeStruct((256, 256), F32)),
        in_specs=[vmem, vmem],
        out_specs=(hbm, hbm),
        scratch_shapes=[dma((2,))],
    )(pltpu.with_memory_space_constraint(sketch, pltpu.VMEM), pltpu.with_memory_space_constraint(gram, pltpu.VMEM))


def hand_out(sketch, gram, sketch_out, gram_out, sem):
    first = pltpu.make_async_copy(gram, gram_out, sem.at[0])
    second = pltpu.make_async_copy(sketch, sketch_out, sem.at[1])
    first.start()
    second.start()
    first.wait()
    second.wait()


def solution(mesh):
    placed = (P(("wide", "narrow"), None), P(("wide", "narrow")), P())
    return jax.shard_map(
        on_device,
        mesh=mesh,
        in_specs=placed,
        out_specs=(P(("wide", "narrow"), None), P()),
        check_vma=False,
    )
```

```python
import functools

import jax
import jax.numpy as jnp
from jax import lax
from jax.experimental import pallas as pl
from jax.experimental.pallas import tpu as pltpu
from jax.sharding import PartitionSpec as P

MESH = pl.DeviceIdType.MESH
PARTS, LEVEL_PARTS = 5, [1, 3]
SQUARE_ROWS, LEVEL_ROWS = 16, 16
SQUARE_PARTS = [a for a in range(PARTS) if a not in LEVEL_PARTS]
SIZES = [128 if a in LEVEL_PARTS else 256 for a in range(PARTS)]
STARTS = [sum(SIZES[:a]) for a in range(PARTS)]
ORDER = tuple((stage, a) for stage in range(3) for a in range(PARTS))
PAIR, SUM, ACROSS, ROUND, HALF = range(5)
PLANE = (
    (2, 2), (1, 2), (2, 1), (3, 2), (2, 3), (1, 1), (3, 3), (1, 3), (3, 1), (0, 2), (2, 0), (0, 1), (1, 0), (0, 3), (3, 0),
)
BY_START = tuple(sorted(range(16), key=lambda q: (min(q // 4, 4 - q // 4) + min(q % 4, 4 - q % 4), q)))
LINE = (4, 3, 5, 2, 6, 1, 7)
BF16, F32, I32 = jnp.bfloat16, jnp.float32, jnp.int32


def contract_rows(a, b):
    return lax.dot_general(a, b, (((0,), (0,)), ((), ())), preferred_element_type=F32)


def split(values):
    hi = values.astype(BF16)
    return hi, (values - hi.astype(F32)).astype(BF16)


def kernel(
    design, flips, ids, sketch_out, gram_out,
    rows_in, flips_in, ids_in, rows_hi, rows_lo, square_signs, level_signs, mine, partner, from_partner, all_sums,
    plane_in, line_across, line_in, plane_across, gathered,
    load_sem, send_sem, recv_sem,
):
    wide, z = lax.axis_index("wide"), lax.axis_index("narrow")
    core, square = lax.rem(wide, 2), lax.div(wide, 2)
    x, y = lax.div(square, 4), lax.rem(square, 4)
    device = wide * 8 + z
    load_ids = pltpu.make_async_copy(ids, ids_in, load_sem.at[0])
    load_ids.start()
    load = pltpu.make_async_copy(design, rows_in, load_sem.at[1])
    load.start()
    load_flips = pltpu.make_async_copy(flips, flips_in, load_sem.at[2])
    load_flips.start()

    squares = [lax.rem(x + dx, 4) * 4 + lax.rem(y + dy, 4) for dx, dy in PLANE]
    plane = [(there * 2 + core, z) for there in squares]
    levels = [lax.rem(z + dz, 8) for dz in LINE]
    line = [(wide, there) for there in levels]
    sibling = (wide + 1 - 2 * core, z)
    rank = sum(jnp.where(square == there, p, 0) for p, there in enumerate(BY_START))
    early_squares = [jnp.where(k < rank, BY_START[k], BY_START[k + 1]) for k in range(15)]
    early_plane = [(there * 2 + core, z) for there in early_squares]
    early_line = [(wide, jnp.where(k < z, k, k + 1)) for k in range(7)]
    barrier = pltpu.get_barrier_semaphore()
    peers = plane + line + [sibling]
    for peer in peers:
        pl.semaphore_signal(barrier, inc=1, device_id=peer, device_id_type=MESH)

    def copy_of(step, a, source, target, peer):
        return pltpu.make_async_remote_copy(
            source, target, send_sem.at[step], recv_sem.at[step, a], device_id=peer, device_id_type=MESH
        )

    bit = lax.broadcasted_iota(I32, (32, 512), 0)
    lane = lax.broadcasted_iota(I32, (32, 512), 1)
    block, low = lax.shift_right_logical(lane, 7), lane & 127
    of_low = lax.shift_right_logical(low, jnp.minimum(bit, 7)) & 1
    of_device = lax.shift_right_logical(jnp.full((32, 512), device, I32), jnp.maximum(bit - 10, 0)) & 1
    of_device = jnp.where(bit >= 10, of_device, 0)
    first = jnp.where(bit < 7, of_low, of_device)
    masks = jnp.where(block == 0, first, jnp.where(bit == 6 + block, 1, 0)).astype(F32).astype(BF16)
    load_ids.wait()
    bit = lax.broadcasted_iota(I32, (32, 1024), 0)
    bits = (lax.shift_right_logical(jnp.broadcast_to(ids_in[...], (32, 1024)), bit) & 1).astype(F32).astype(BF16)
    counts = contract_rows(bits, masks)
    base = (1 - 2 * (counts[:, :128].astype(I32) & 1)).astype(F32)
    for j in range(4):
        sign = (base if j == 0 else 1.0 - 2.0 * counts[:, 128 * j : 128 * j + 128]).astype(BF16)
        square_signs[j] = sign[:768].reshape(16, 3, SQUARE_ROWS, 128)
        level_signs[j] = sign[768:].reshape(2, 128, 128)

    load_flips.wait()
    flip = flips_in[...].astype(F32).astype(BF16)
    load.wait()
    hi, lo = split(rows_in[...] * (1.0 / 512.0))
    rows_hi[...] = hi
    rows_lo[...] = lo

    def signs_of(a, j):
        if a in LEVEL_PARTS:
            return level_signs[j, LEVEL_PARTS.index(a)]
        return square_signs[j, :, SQUARE_PARTS.index(a)].reshape(256, 128)

    for a in range(PARTS):
        table = [signs_of(a, 0)]
        for j in (1, 2, 3):
            other = signs_of(a, j)
            table = table + [s * other for s in table]
        table = [s * jnp.broadcast_to(flip[:, 128 * k : 128 * k + 128], (SIZES[a], 128)) for k, s in enumerate(table)]
        table = jnp.concatenate(table, axis=1)
        got = jnp.dot(table, rows_hi[...], preferred_element_type=F32)
        got = got + jnp.dot(table, rows_lo[...], preferred_element_type=F32)
        left, right = got[:, :128], got[:, 128:]
        mine[a, : SIZES[a]] = jnp.where(core == 0, left, right)
        partner[a, : SIZES[a]] = jnp.where(core == 0, right, left)
    pl.semaphore_wait(barrier, len(peers))
    for a in range(PARTS):
        rows = pl.ds(0, SIZES[a])
        copy_of(PAIR, a, partner.at[a, rows], from_partner.at[a, rows], sibling).start()

    def of_square(there, first=0):
        return pl.ds(pl.multiple_of(first + there * SQUARE_ROWS, 8), SQUARE_ROWS)

    def of_level(there, first=0):
        return pl.ds(pl.multiple_of(first + there * LEVEL_ROWS, 8), LEVEL_ROWS)

    def all_of(step, a):
        if step == PAIR:
            whole = from_partner.at[a, pl.ds(0, SIZES[a])]
        elif step == HALF:
            whole = gathered.at[0, a, pl.ds(0, SIZES[a])]
        elif a in LEVEL_PARTS:
            b = LEVEL_PARTS.index(a)
            whole = (line_in.at[b], plane_across.at[b, pl.ds(0, 15)], gathered.at[0, a, pl.ds(0, 7 * LEVEL_ROWS)])[step - SUM]
        else:
            b = SQUARE_PARTS.index(a)
            whole = (
                plane_in.at[b], line_across.at[b, pl.ds(0, 7)], gathered.at[0, a, pl.ds(0, 15 * SQUARE_ROWS)]
            )[step - SUM]
        return copy_of(step, a, whole, whole, sibling)

    for a in range(PARTS):
        all_of(PAIR, a).wait_recv()
        all_sums[pl.ds(STARTS[a], SIZES[a])] = mine[a, : SIZES[a]] + from_partner[a, : SIZES[a]]
        if a in LEVEL_PARTS:
            b = LEVEL_PARTS.index(a)
            for n in range(7):
                copy_of(SUM, a, all_sums.at[of_level(levels[n], STARTS[a])], line_in.at[b, n], line[n]).start()
        else:
            b = SQUARE_PARTS.index(a)
            for n in range(15):
                copy_of(SUM, a, all_sums.at[of_square(squares[n], STARTS[a])], plane_in.at[b, n], plane[n]).start()
    def add_up(a):
        all_of(SUM, a).wait_recv()
        if a in LEVEL_PARTS:
            b = LEVEL_PARTS.index(a)
            total = all_sums[of_level(z, STARTS[a])]
            for n in range(7):
                total = total + line_in[b, n]
            plane_across[b, square] = total
            here = plane_across.at[b, square]
            for n in range(15):
                copy_of(ACROSS, a, here, here, plane[n]).start()
        else:
            b = SQUARE_PARTS.index(a)
            total = all_sums[of_square(square, STARTS[a])]
            for n in range(15):
                total = total + plane_in[b, n]
            line_across[b, z] = total
            here = line_across.at[b, z]
            for n in range(7):
                copy_of(ACROSS, a, here, here, early_line[n]).start()

    def add_across(a):
        all_of(ACROSS, a).wait_recv()
        if a in LEVEL_PARTS:
            b = LEVEL_PARTS.index(a)
            terms, own, others = [plane_across[b, k] for k in range(16)], of_level(z), early_line
        else:
            b = SQUARE_PARTS.index(a)
            terms, own, others = [line_across[b, k] for k in range(8)], of_square(square), early_plane
        total = terms[0]
        for term in terms[1:]:
            total = total + term
        gathered[core, a, own] = total
        here = gathered.at[core, a, own]
        for peer in others:
            copy_of(ROUND, a, here, here, peer).start()

    def pass_on(a):
        all_of(ROUND, a).wait_recv()
        here = gathered.at[core, a, pl.ds(0, SIZES[a])]
        copy_of(HALF, a, here, here, sibling).start()

    for stage, a in ORDER:
        (add_up, add_across, pass_on)[stage](a)
    gram = None
    for a in range(PARTS):
        all_of(HALF, a).wait_recv()
        left, right = gathered[0, a, : SIZES[a]], gathered[1, a, : SIZES[a]]
        hi, lo = split(jnp.concatenate([left, right], axis=1))
        cross = contract_rows(hi, lo)
        term = contract_rows(hi, hi) + (cross + cross.T)
        gram = term if gram is None else gram + term
    gram_out[...] = gram * (1.0 / 1024.0)
    row = device * 4
    b = lax.div(lax.rem(row, 48), 16)
    in_square = lax.div(row, 48) * SQUARE_ROWS + lax.rem(row, 16)
    in_level = jnp.maximum(row - 768, 0)
    part = jnp.where(row < 768, 2 * b, 1 + 2 * lax.div(in_level, 128))
    tile = pl.ds(pl.multiple_of(lax.div(jnp.where(row < 768, in_square, lax.rem(in_level, 128)), 8) * 8, 8), 8)
    for h in range(2):
        eight = gathered[h, part, tile]
        sketch_out[:, 128 * h : 128 * h + 128] = jnp.where(lax.rem(z, 2) == 0, eight[:4], eight[4:])
    for step, rows in enumerate((1024, 944, 816, 944, 1024)):
        whole = all_sums.at[pl.ds(0, rows)]
        copy_of(step, 0, whole, whole, sibling).wait_send()


def on_device(design, sign_flips, sample_ids):
    dma = pltpu.SemaphoreType.DMA
    vmem, hbm = pl.BlockSpec(memory_space=pltpu.VMEM), pl.BlockSpec(memory_space=pltpu.HBM)
    sketch, gram = pl.pallas_call(
        kernel,
        out_shape=(pltpu.VMEM((4, 256), F32), pltpu.VMEM((256, 256), F32)),
        in_specs=[hbm, hbm, hbm],
        out_specs=(vmem, vmem),
        scratch_shapes=[
            pltpu.VMEM((1024, 256), F32),
            pltpu.VMEM((1, 1024), I32),
            pltpu.VMEM((1, 1024), I32),
            pltpu.VMEM((1024, 256), BF16),
            pltpu.VMEM((1024, 256), BF16),
            pltpu.VMEM((4, 16, 3, SQUARE_ROWS, 128), BF16),
            pltpu.VMEM((4, 2, 128, 128), BF16),
            pltpu.VMEM((PARTS, 256, 128), F32),
            pltpu.VMEM((PARTS, 256, 128), F32),
            pltpu.VMEM((PARTS, 256, 128), F32),
            pltpu.VMEM((1024, 128), F32),
            pltpu.VMEM((3, 15, SQUARE_ROWS, 128), F32),
            pltpu.VMEM((3, 8, SQUARE_ROWS, 128), F32),
            pltpu.VMEM((2, 7, LEVEL_ROWS, 128), F32),
            pltpu.VMEM((2, 16, LEVEL_ROWS, 128), F32),
            pltpu.VMEM((2, PARTS, 256, 128), F32),
            dma((3,)), dma((5,)), dma((5, PARTS)),
        ],
        compiler_params=pltpu.CompilerParams(collective_id=0, has_side_effects=True, vmem_limit_bytes=40 << 20),
    )(*[pltpu.with_memory_space_constraint(v, pltpu.HBM) for v in (design, sign_flips.reshape(1, 1024), sample_ids.reshape(1, 1024))])
    return pl.pallas_call(
        hand_out,
        out_shape=(jax.ShapeDtypeStruct((4, 256), F32), jax.ShapeDtypeStruct((256, 256), F32)),
        in_specs=[vmem, vmem],
        out_specs=(hbm, hbm),
        scratch_shapes=[dma((2,))],
    )(pltpu.with_memory_space_constraint(sketch, pltpu.VMEM), pltpu.with_memory_space_constraint(gram, pltpu.VMEM))


def hand_out(sketch, gram, sketch_out, gram_out, sem):
    first = pltpu.make_async_copy(gram, gram_out, sem.at[0])
    second = pltpu.make_async_copy(sketch, sketch_out, sem.at[1])
    first.start()
    second.start()
    first.wait()
    second.wait()


def solution(mesh):
    placed = (P(("wide", "narrow"), None), P(("wide", "narrow")), P())
    return jax.shard_map(
        on_device,
        mesh=mesh,
        in_specs=placed,
        out_specs=(P(("wide", "narrow"), None), P()),
        check_vma=False,
    )
```

```python
import functools

import jax
import jax.numpy as jnp
from jax import lax
from jax.experimental import pallas as pl
from jax.experimental.pallas import tpu as pltpu
from jax.sharding import PartitionSpec as P

MESH = pl.DeviceIdType.MESH
PARTS, LEVEL_PARTS = 5, [1, 3]
SQUARE_ROWS, LEVEL_ROWS = 16, 16
SQUARE_PARTS = [a for a in range(PARTS) if a not in LEVEL_PARTS]
SIZES = [128 if a in LEVEL_PARTS else 256 for a in range(PARTS)]
STARTS = [sum(SIZES[:a]) for a in range(PARTS)]
ORDER = tuple((stage, a) for stage in range(3) for a in range(PARTS))
PAIR, SUM, ACROSS, ROUND, HALF = range(5)
PLANE = (
    (2, 2), (1, 2), (2, 1), (3, 2), (2, 3), (1, 1), (3, 3), (1, 3), (3, 1), (0, 2), (2, 0), (0, 1), (1, 0), (0, 3), (3, 0),
)
BY_START = tuple(sorted(range(16), key=lambda q: (min(q // 4, 4 - q // 4) + min(q % 4, 4 - q % 4), q)))
LINE = (4, 3, 5, 2, 6, 1, 7)
BF16, F32, I32 = jnp.bfloat16, jnp.float32, jnp.int32


def contract_rows(a, b):
    return lax.dot_general(a, b, (((0,), (0,)), ((), ())), preferred_element_type=F32)


def split(values):
    hi = values.astype(BF16)
    return hi, (values - hi.astype(F32)).astype(BF16)


def kernel(
    design, flips, ids, sketch_out, gram_out,
    rows_in, flips_in, ids_in, rows_hi, rows_lo, square_signs, level_signs, mine, partner, from_partner, all_sums,
    plane_in, line_across, line_in, plane_across, gathered,
    load_sem, send_sem, recv_sem,
):
    wide, z = lax.axis_index("wide"), lax.axis_index("narrow")
    core, square = lax.rem(wide, 2), lax.div(wide, 2)
    x, y = lax.div(square, 4), lax.rem(square, 4)
    device = wide * 8 + z
    load_ids = pltpu.make_async_copy(ids, ids_in, load_sem.at[0])
    load_ids.start()
    quarters = [pl.ds(256 * k, 256) for k in range(4)]
    loads = [pltpu.make_async_copy(design.at[q], rows_in.at[q], load_sem.at[2 + k]) for k, q in enumerate(quarters)]
    for load in loads:
        load.start()
    load_flips = pltpu.make_async_copy(flips, flips_in, load_sem.at[1])
    load_flips.start()

    squares = [lax.rem(x + dx, 4) * 4 + lax.rem(y + dy, 4) for dx, dy in PLANE]
    plane = [(there * 2 + core, z) for there in squares]
    levels = [lax.rem(z + dz, 8) for dz in LINE]
    line = [(wide, there) for there in levels]
    sibling = (wide + 1 - 2 * core, z)
    rank = sum(jnp.where(square == there, p, 0) for p, there in enumerate(BY_START))
    early_squares = [jnp.where(k < rank, BY_START[k], BY_START[k + 1]) for k in range(15)]
    early_plane = [(there * 2 + core, z) for there in early_squares]
    early_line = [(wide, jnp.where(k < z, k, k + 1)) for k in range(7)]
    barrier = pltpu.get_barrier_semaphore()
    peers = plane + line + [sibling]
    for peer in peers:
        pl.semaphore_signal(barrier, inc=1, device_id=peer, device_id_type=MESH)

    def copy_of(step, a, source, target, peer):
        return pltpu.make_async_remote_copy(
            source, target, send_sem.at[step], recv_sem.at[step, a], device_id=peer, device_id_type=MESH
        )

    bit = lax.broadcasted_iota(I32, (32, 512), 0)
    lane = lax.broadcasted_iota(I32, (32, 512), 1)
    block, low = lax.shift_right_logical(lane, 7), lane & 127
    of_low = lax.shift_right_logical(low, jnp.minimum(bit, 7)) & 1
    of_device = lax.shift_right_logical(jnp.full((32, 512), device, I32), jnp.maximum(bit - 10, 0)) & 1
    of_device = jnp.where(bit >= 10, of_device, 0)
    first = jnp.where(bit < 7, of_low, of_device)
    masks = jnp.where(block == 0, first, jnp.where(bit == 6 + block, 1, 0)).astype(F32).astype(BF16)
    load_ids.wait()
    bit = lax.broadcasted_iota(I32, (32, 1024), 0)
    bits = (lax.shift_right_logical(jnp.broadcast_to(ids_in[...], (32, 1024)), bit) & 1).astype(F32).astype(BF16)
    counts = contract_rows(bits, masks)
    base = (1 - 2 * (counts[:, :128].astype(I32) & 1)).astype(F32)
    for j in range(4):
        sign = (base if j == 0 else 1.0 - 2.0 * counts[:, 128 * j : 128 * j + 128]).astype(BF16)
        square_signs[j] = sign[:768].reshape(16, 3, SQUARE_ROWS, 128)
        level_signs[j] = sign[768:].reshape(2, 128, 128)

    load_flips.wait()
    flip = flips_in[...].astype(F32).astype(BF16)
    for load, q in zip(loads, quarters):
        load.wait()
        hi, lo = split(rows_in[q] * (1.0 / 512.0))
        rows_hi[q] = hi
        rows_lo[q] = lo

    def signs_of(a, j):
        if a in LEVEL_PARTS:
            return level_signs[j, LEVEL_PARTS.index(a)]
        return square_signs[j, :, SQUARE_PARTS.index(a)].reshape(256, 128)

    for a in range(PARTS):
        table = [signs_of(a, 0)]
        for j in (1, 2, 3):
            other = signs_of(a, j)
            table = table + [s * other for s in table]
        table = [s * jnp.broadcast_to(flip[:, 128 * k : 128 * k + 128], (SIZES[a], 128)) for k, s in enumerate(table)]
        table = jnp.concatenate(table, axis=1)
        got = jnp.dot(table, rows_hi[...], preferred_element_type=F32)
        got = got + jnp.dot(table, rows_lo[...], preferred_element_type=F32)
        left, right = got[:, :128], got[:, 128:]
        mine[a, : SIZES[a]] = jnp.where(core == 0, left, right)
        partner[a, : SIZES[a]] = jnp.where(core == 0, right, left)
    pl.semaphore_wait(barrier, len(peers))
    for a in range(PARTS):
        rows = pl.ds(0, SIZES[a])
        copy_of(PAIR, a, partner.at[a, rows], from_partner.at[a, rows], sibling).start()

    def of_square(there, first=0):
        return pl.ds(pl.multiple_of(first + there * SQUARE_ROWS, 8), SQUARE_ROWS)

    def of_level(there, first=0):
        return pl.ds(pl.multiple_of(first + there * LEVEL_ROWS, 8), LEVEL_ROWS)

    def all_of(step, a):
        if step == PAIR:
            whole = from_partner.at[a, pl.ds(0, SIZES[a])]
        elif step == HALF:
            whole = gathered.at[0, a, pl.ds(0, SIZES[a])]
        elif a in LEVEL_PARTS:
            b = LEVEL_PARTS.index(a)
            whole = (line_in.at[b], plane_across.at[b, pl.ds(0, 15)], gathered.at[0, a, pl.ds(0, 7 * LEVEL_ROWS)])[step - SUM]
        else:
            b = SQUARE_PARTS.index(a)
            whole = (
                plane_in.at[b], line_across.at[b, pl.ds(0, 7)], gathered.at[0, a, pl.ds(0, 15 * SQUARE_ROWS)]
            )[step - SUM]
        return copy_of(step, a, whole, whole, sibling)

    for a in range(PARTS):
        all_of(PAIR, a).wait_recv()
        all_sums[pl.ds(STARTS[a], SIZES[a])] = mine[a, : SIZES[a]] + from_partner[a, : SIZES[a]]
        if a in LEVEL_PARTS:
            b = LEVEL_PARTS.index(a)
            for n in range(7):
                copy_of(SUM, a, all_sums.at[of_level(levels[n], STARTS[a])], line_in.at[b, n], line[n]).start()
        else:
            b = SQUARE_PARTS.index(a)
            for n in range(15):
                copy_of(SUM, a, all_sums.at[of_square(squares[n], STARTS[a])], plane_in.at[b, n], plane[n]).start()
    def add_up(a):
        all_of(SUM, a).wait_recv()
        if a in LEVEL_PARTS:
            b = LEVEL_PARTS.index(a)
            total = all_sums[of_level(z, STARTS[a])]
            for n in range(7):
                total = total + line_in[b, n]
            plane_across[b, square] = total
            here = plane_across.at[b, square]
            for n in range(15):
                copy_of(ACROSS, a, here, here, plane[n]).start()
        else:
            b = SQUARE_PARTS.index(a)
            total = all_sums[of_square(square, STARTS[a])]
            for n in range(15):
                total = total + plane_in[b, n]
            line_across[b, z] = total
            here = line_across.at[b, z]
            for n in range(7):
                copy_of(ACROSS, a, here, here, early_line[n]).start()

    def add_across(a):
        all_of(ACROSS, a).wait_recv()
        if a in LEVEL_PARTS:
            b = LEVEL_PARTS.index(a)
            terms, own, others = [plane_across[b, k] for k in range(16)], of_level(z), early_line
        else:
            b = SQUARE_PARTS.index(a)
            terms, own, others = [line_across[b, k] for k in range(8)], of_square(square), early_plane
        total = terms[0]
        for term in terms[1:]:
            total = total + term
        gathered[core, a, own] = total
        here = gathered.at[core, a, own]
        for peer in others:
            copy_of(ROUND, a, here, here, peer).start()

    def pass_on(a):
        all_of(ROUND, a).wait_recv()
        here = gathered.at[core, a, pl.ds(0, SIZES[a])]
        copy_of(HALF, a, here, here, sibling).start()

    for stage, a in ORDER:
        (add_up, add_across, pass_on)[stage](a)
    gram = None
    for a in range(PARTS):
        all_of(HALF, a).wait_recv()
        left, right = gathered[0, a, : SIZES[a]], gathered[1, a, : SIZES[a]]
        hi, lo = split(jnp.concatenate([left, right], axis=1))
        term = contract_rows(hi, hi) + (contract_rows(hi, lo) + contract_rows(lo, hi))
        gram = term if gram is None else gram + term
    gram_out[...] = gram * (1.0 / 1024.0)
    row = device * 4
    b = lax.div(lax.rem(row, 48), 16)
    in_square = lax.div(row, 48) * SQUARE_ROWS + lax.rem(row, 16)
    in_level = jnp.maximum(row - 768, 0)
    part = jnp.where(row < 768, 2 * b, 1 + 2 * lax.div(in_level, 128))
    tile = pl.ds(pl.multiple_of(lax.div(jnp.where(row < 768, in_square, lax.rem(in_level, 128)), 8) * 8, 8), 8)
    for h in range(2):
        eight = gathered[h, part, tile]
        sketch_out[:, 128 * h : 128 * h + 128] = jnp.where(lax.rem(z, 2) == 0, eight[:4], eight[4:])
    for step, rows in enumerate((1024, 944, 816, 944, 1024)):
        whole = all_sums.at[pl.ds(0, rows)]
        copy_of(step, 0, whole, whole, sibling).wait_send()


def on_device(design, sign_flips, sample_ids):
    dma = pltpu.SemaphoreType.DMA
    vmem, hbm = pl.BlockSpec(memory_space=pltpu.VMEM), pl.BlockSpec(memory_space=pltpu.HBM)
    sketch, gram = pl.pallas_call(
        kernel,
        out_shape=(pltpu.VMEM((4, 256), F32), pltpu.VMEM((256, 256), F32)),
        in_specs=[hbm, hbm, hbm],
        out_specs=(vmem, vmem),
        scratch_shapes=[
            pltpu.VMEM((1024, 256), F32),
            pltpu.VMEM((1, 1024), I32),
            pltpu.VMEM((1, 1024), I32),
            pltpu.VMEM((1024, 256), BF16),
            pltpu.VMEM((1024, 256), BF16),
            pltpu.VMEM((4, 16, 3, SQUARE_ROWS, 128), BF16),
            pltpu.VMEM((4, 2, 128, 128), BF16),
            pltpu.VMEM((PARTS, 256, 128), F32),
            pltpu.VMEM((PARTS, 256, 128), F32),
            pltpu.VMEM((PARTS, 256, 128), F32),
            pltpu.VMEM((1024, 128), F32),
            pltpu.VMEM((3, 15, SQUARE_ROWS, 128), F32),
            pltpu.VMEM((3, 8, SQUARE_ROWS, 128), F32),
            pltpu.VMEM((2, 7, LEVEL_ROWS, 128), F32),
            pltpu.VMEM((2, 16, LEVEL_ROWS, 128), F32),
            pltpu.VMEM((2, PARTS, 256, 128), F32),
            dma((6,)), dma((5,)), dma((5, PARTS)),
        ],
        compiler_params=pltpu.CompilerParams(collective_id=0, has_side_effects=True, vmem_limit_bytes=40 << 20),
    )(*[pltpu.with_memory_space_constraint(v, pltpu.HBM) for v in (design, sign_flips.reshape(1, 1024), sample_ids.reshape(1, 1024))])
    return pl.pallas_call(
        hand_out,
        out_shape=(jax.ShapeDtypeStruct((4, 256), F32), jax.ShapeDtypeStruct((256, 256), F32)),
        in_specs=[vmem, vmem],
        out_specs=(hbm, hbm),
        scratch_shapes=[dma((2,))],
    )(pltpu.with_memory_space_constraint(sketch, pltpu.VMEM), pltpu.with_memory_space_constraint(gram, pltpu.VMEM))


def hand_out(sketch, gram, sketch_out, gram_out, sem):
    first = pltpu.make_async_copy(gram, gram_out, sem.at[0])
    second = pltpu.make_async_copy(sketch, sketch_out, sem.at[1])
    first.start()
    second.start()
    first.wait()
    second.wait()


def solution(mesh):
    placed = (P(("wide", "narrow"), None), P(("wide", "narrow")), P())
    return jax.shard_map(
        on_device,
        mesh=mesh,
        in_specs=placed,
        out_specs=(P(("wide", "narrow"), None), P()),
        check_vma=False,
    )
```
